32 devices in a mesh: ens: 2 (over x), tile: 16 (over z, y, core).
Axes of the slice: x: 2, y: 2, z: 4, core: 2. Of those that a mesh axis runs over, the one named last changes fastest.
Arguments:
- departure: float32 [131072], P(('ens', 'tile')), parts along dimension 0, may hold values from -6 to 6
- obs_weight: float32 [131072], P(('ens', 'tile')), parts along dimension 0, may hold values from 1 to 10
- owner_id: int32 [131072, 1], P(('ens', 'tile')), parts along dimension 0, may hold values from 0 to 15; in each aligned block of 4096 rows (0 to 4095, 4096 to 8191, ...) at most 512 rows name the same one
- obs_level: int32 [131072], P(('ens', 'tile')), parts along dimension 0, may hold values from 0 to 126
- columns: int32 [4, 131072], P(None, ('ens', 'tile')), parts along dimension 1, may hold values from 0 to 4095, as said below
- interp_weight: float32 [4, 131072], P(None, ('ens', 'tile')), parts along dimension 1, may hold values from 0 to 1, as said below
- vert_root: float32 [127, 127], replicated, may hold values from -0.5 to 0.5
- spread: float32 [256, 256], P('tile'), may hold values from 0.05 to 0.24
- lanczos: float32 [127, 512, 256], P(None, ('ens', 'tile')), parts along dimension 1, may hold values from -70 to 70
- previous: float32 [127, 512, 256], P(None, ('ens', 'tile')), parts along dimension 1, may hold values from -6 to 6
- beta_prev: float32 [2], P('ens'), parts along dimension 0, may hold values from 0.3 to 1.5
Outputs:
- next_vector: float32 [127, 512, 256], P(None, ('ens', 'tile')), parts along dimension 1
- coefficients: float32 [4], P('ens'), parts along dimension 0
The draws below stay inside these ranges and needn't reach their ends.
There are 2 independent parts, one for each index of `ens`. The reference program is written for one: setup_inputs(seed, part) draws one part's arguments, and reference() takes and returns one part's arrays. A program takes and returns all parts, laid end to end along the dimension named above; an argument that names none is the same for every part. Nothing has to cross between parts.
Inputs may be any that keep to these rules, and one draw needn't show every extreme that they name: `owner_id`: in the rows of one device at most 512 observations name one owner; some owner is named by exactly 512 of them. `columns`: the four entries of an observation are the corners of one cell of the owner's rows, in the order (i, j), (i, j + 1), (i + 1, j), (i + 1, j + 1) with j + 1 taken modulo 256; an entry is i * 256 + j. `interp_weight`: bilinear weights: the four of an observation sum to one.
All inputs are finite; a program needn't handle non-finite values.
Results may differ from the reference program's by a relative error of at most 0.0003.
Values sent between devices are 32-bit elements; how exact they have to be, the bound alone decides.
A program may use at most 64 MiB of HBM per device.

```python
import math
import jax
import jax.numpy as jnp
import numpy as np
from jax import lax

LEV = 127
SWEEPS = 4
RX = 16
NY = 256
OBS_DEV = 4096
CAP = 512
NXG = 256
OBS = 65536
N_TILE = 16


def draw_columns(key, part):
    key = jax.random.fold_in(key, 5)
    first, second = jax.random.split(key)
    base_row = jax.random.randint(first, (OBS,), 0, RX - 1)
    base_col = jax.random.randint(second, (OBS,), 0, NY)
    next_col = (base_col + 1) % NY
    return jnp.stack([base_row * NY + base_col, base_row * NY + next_col, (base_row + 1) * NY + base_col, (base_row + 1) * NY + next_col]).astype(jnp.int32)


def draw_interp_weight(key, part):
    key = jax.random.fold_in(key, 7)
    first, second = jax.random.split(key)
    frac_x = jax.random.uniform(first, (OBS,), jnp.float32)
    frac_y = jax.random.uniform(second, (OBS,), jnp.float32)
    return jnp.stack([(1.0 - frac_x) * (1.0 - frac_y), (1.0 - frac_x) * frac_y, frac_x * (1.0 - frac_y), frac_x * frac_y])


def draw_lanczos(key, part):
    key = jax.random.fold_in(key, 11)
    first, second, third = jax.random.split(key, 3)
    position = jnp.arange(NXG, dtype=jnp.float32) / NXG
    row_scale = jnp.exp(0.5 * math.log(10.0) * jax.random.uniform(second, (NXG,), jnp.float32))
    col_scale = jnp.exp(0.5 * math.log(10.0) * jax.random.uniform(third, (NY,), jnp.float32))
    base = jnp.clip(jax.random.normal(first, (LEV, NXG, NY), jnp.float32), -4.0, 4.0)
    trend = jnp.power(3.0, 0.5 * position)
    return base * (row_scale * trend)[None, :, None] * col_scale[None, None, :]


def set_ends(values, rng, low, top_value):
    shape = values.shape
    place = [jax.random.randint(jax.random.fold_in(rng, axis), (), 0, shape[axis]) for axis in range(len(shape))]
    values = values.at[tuple(place)].set(low)
    longest = shape.index(max(shape))
    place[longest] = (place[longest] + 1) % shape[longest]
    return values.at[tuple(place)].set(top_value)


def steps_of(stream_key, extent, cuts, least, high):
    factor_of = 1.0
    for axis_at, blocks in cuts:
        draws = jax.random.uniform(jax.random.fold_in(jax.random.fold_in(stream_key, 6), axis_at), (blocks,), jnp.float32, least / len(cuts), high / len(cuts))
        factor_of = factor_of * jnp.repeat(jnp.exp(draws), extent[axis_at] // blocks).reshape((-1,) + (1,) * (len(extent) - 1 - axis_at))
    return factor_of


def shared_out(key, own, number, rows, amount, top, most, skew):
    ranking = jax.random.permutation(key, amount)
    crowded, usual = load_shares(amount, rows * top, most, skew, True), load_shares(amount, rows * top, most, skew, False)
    places = jnp.arange(amount)

    def named(tallies, turn):
        used = int((tallies > 0).sum())
        fixed = max(1, used // 4)
        shifted = fixed + (places - fixed + turn * (used - fixed)) % max(1, amount - fixed)
        return jnp.zeros((amount,), jnp.int32).at[ranking[jnp.where(places < fixed, places, shifted)]].set(jnp.asarray(tallies, jnp.int32))

    tallies = jnp.where(number % 4 == 0, named(crowded, number // 4), named(usual, number - number // 4 - 1))
    mixed = jax.random.permutation(jax.random.fold_in(own, 3), amount)
    donor, receiver = mixed[0:amount // 2 * 2:2], mixed[1:amount // 2 * 2:2]
    room = jnp.minimum(tallies[donor] - 1, most - tallies[receiver]) // 2
    room = jnp.where((donor == ranking[0]) | (receiver == ranking[0]) | (tallies[receiver] == 0), 0, jnp.maximum(room, 0))
    shifted = jax.random.randint(jax.random.fold_in(own, 4), (amount // 2,), 0, 1 << 20) % (room + 1)
    tallies = tallies.at[donor].add(-shifted).at[receiver].add(shifted)
    members = jnp.searchsorted(jnp.cumsum(tallies), jnp.arange(rows * top), side="right").astype(jnp.int32)
    table = members.reshape(top, rows).T
    table = table[jax.random.permutation(jax.random.fold_in(own, 1), rows)]
    turn = jax.random.randint(jax.random.fold_in(own, 2), (rows, 1), 0, top)
    return jnp.take_along_axis(table, (jnp.arange(top)[None, :] + turn) % top, axis=1)


def load_shares(count, total, bound, slope, full):
    loads = [(1 << 20) // math.isqrt(standing ** slope) + 1 for standing in range(1, count + 1)]
    largest = bound if full else min(bound, max(-(-total // count), total * loads[0] // sum(loads)))
    least = 1 if total - largest >= count - 1 else 0
    given, spare = [largest] + [least] * (count - 1), total - largest - least * (count - 1)
    while spare > 0:
        candidates = [i for i in range(1, count) if given[i] < largest] or [i for i in range(1, count) if given[i] < bound]
        whole, left = sum([loads[i] for i in candidates]), spare
        for i in candidates:
            more = min(bound - given[i], max(1, left * loads[i] // whole), spare)
            given[i] = given[i] + more
            spare = spare - more
    return np.array(given)


def scatter_about(own_key, shape, deviation, reach, pieces=(), held_as=jnp.bfloat16):
    drawn = deviation * jax.random.normal(own_key, shape, jnp.float32)
    if pieces:
        drawn = drawn * steps_of(own_key, shape, pieces, -0.22, 0.18)
    return jnp.clip(drawn, -reach, reach).astype(held_as)


def setup_inputs(seed: int = 0, part: int = 0) -> dict:
    streams_of = jax.random.split(jax.random.key(seed), 12)
    part_splits = jax.random.split(jax.random.fold_in(streams_of[11], part), 12)
    departure = scatter_about(part_splits[0], (OBS,), 1.0, 6.0, ((0, 16),), jnp.float32)
    obs_weight = jnp.clip(jnp.exp(math.log(10.0) - 2.3025851 * jax.random.uniform(part_splits[1], (OBS,), jnp.float32) ** steps_of(part_splits[1], (OBS,), ((0, 16),), -0.2, 0.2)), 1.0, 10.0)
    owner_id_keys = jax.random.split(jax.random.fold_in(part_splits[2], 1), OBS // OBS_DEV)
    owner_id_turns = jax.random.permutation(jax.random.fold_in(part_splits[2], 3), OBS // OBS_DEV)
    owner_id = jax.vmap(lambda own, number: shared_out(jax.random.fold_in(part_splits[2], 2), own, number, OBS_DEV, N_TILE, 1, CAP, 2))(owner_id_keys, owner_id_turns).reshape((OBS, 1))
    obs_level = set_ends(jax.random.randint(part_splits[3], (OBS,), 0, LEV), jax.random.fold_in(part_splits[3], 1), 0, LEV - 1).astype(jnp.int32)
    columns = draw_columns(jax.random.fold_in(jax.random.fold_in(streams_of[11], part), 71), part)
    interp_weight = draw_interp_weight(jax.random.fold_in(jax.random.fold_in(streams_of[11], part), 71), part)
    vert_root = scatter_about(streams_of[6], (LEV, LEV), LEV ** -0.5, 0.5, (), jnp.float32)
    spread = jnp.clip(jnp.exp(math.log(0.24) - 1.5686159 * jax.random.uniform(streams_of[7], (NXG, NY), jnp.float32) ** steps_of(streams_of[7], (NXG, NY), ((0, 16),), -0.2, 0.2)), 0.05, 0.24)
    lanczos = draw_lanczos(jax.random.fold_in(jax.random.fold_in(streams_of[11], part), 71), part)
    previous = scatter_about(part_splits[9], (LEV, NXG, NY), 1.0, 6.0, ((1, 16),), jnp.float32)
    beta_prev = jnp.clip(jnp.exp(jax.random.uniform(part_splits[10], (1,), jnp.float32, math.log(0.3), math.log(1.5))), 0.3, 1.5)
    return {"departure": departure, "obs_weight": obs_weight, "owner_id": owner_id, "obs_level": obs_level, "columns": columns, "interp_weight": interp_weight, "vert_root": vert_root, "spread": spread, "lanczos": lanczos, "previous": previous, "beta_prev": beta_prev}


HIGH = lax.Precision.HIGHEST

def smooth_sweeps(field, spread):
    for sweep in range(SWEEPS):
        pushed = spread[None] * field
        padded = jnp.pad(pushed, ((0, 0), (1, 1), (0, 0)))
        laplace = padded[:, 2:] + padded[:, :-2] + jnp.roll(pushed, 1, 2) + jnp.roll(pushed, -1, 2) - 4.0 * pushed
        field = field + laplace
    return field

def reference(departure, obs_weight, owner_id, obs_level, columns, interp_weight, vert_root, spread, lanczos, previous, beta_prev):
    block_cells = RX * NY
    total_cells = NXG * NY
    weighted = obs_weight * departure
    contrib = (interp_weight * weighted[None, :]).reshape(-1)
    target = (obs_level[None, :] * total_cells + owner_id[:, 0][None, :] * block_cells + columns).astype(jnp.int32).reshape(-1)
    gradient = jnp.zeros((LEV * total_cells,), jnp.float32).at[target].add(contrib).reshape(LEV, total_cells)
    vertical = jnp.dot(vert_root.T, gradient, precision=HIGH, preferred_element_type=jnp.float32)
    smoothed = smooth_sweeps(vertical.reshape(LEV, NXG, NY), spread)
    combined = lanczos + smoothed - beta_prev[0] * previous
    self_square = jnp.sum(lanczos * lanczos)
    alpha = jnp.sum(combined * lanczos) / self_square
    remainder = combined - alpha * lanczos
    beta = jnp.sqrt(jnp.sum(remainder * remainder) / self_square + 1e-06)
    return (remainder / beta, jnp.stack([alpha, beta]))
```

```python
import functools

import jax
import jax.numpy as jnp
from jax import lax
from jax.experimental import pallas as pl
from jax.experimental.pallas import tpu as pltpu
from jax.sharding import PartitionSpec as P

SWEEPS = 4
GROUP = 512
F32 = jnp.float32
BF16 = jnp.bfloat16
HIGH = lax.Precision.HIGHEST
MESH = pl.DeviceIdType.MESH
VMEM_LIMIT = 48 * 1024 * 1024


def iota(shape, axis):
    return lax.broadcasted_iota(jnp.int32, shape, axis)


def dot_nt(a, b):
    return lax.dot_general(a, b, (((1,), (1,)), ((), ())), preferred_element_type=F32)


def split(x):
    hi = x.astype(BF16).astype(F32)
    return hi, x - hi


def earlier(size):
    return (iota((size, size), 0) < iota((size, size), 1)).astype(BF16)


def greet(tiles, me, ens):
    barrier = pltpu.get_barrier_semaphore()

    def signal(k, carry):
        peer = lax.rem(me + k, tiles)
        pl.semaphore_signal(barrier, inc=1, device_id=(ens, peer), device_id_type=MESH)
        return carry

    lax.fori_loop(1, tiles, signal, 0)
    return barrier


def route_kernel(
    tiles, cap, dep_ref, wgt_ref, own_ref, lev_ref, col_ref, itp_ref, out_ref,
    rank_ref, pay_ref, send_ref, send_sem, recv_sem,
):
    me, ens = lax.axis_index("tile"), lax.axis_index("ens")
    barrier = greet(tiles, me, ens)
    obs = dep_ref.shape[1]
    size = 256
    upper = earlier(size)
    base = jnp.zeros((tiles, 1), F32)
    for c in range(obs // size):
        at = pl.ds(c * size, size)
        hot = own_ref[:, at] == iota((tiles, size), 0)
        one = hot.astype(F32)
        before = jnp.dot(one.astype(BF16), upper, preferred_element_type=F32)
        rank_ref[:, at] = jnp.sum(one * (before + base), axis=0, keepdims=True).astype(jnp.int32)
        base = base + jnp.sum(one, axis=1, keepdims=True)
        value = itp_ref[:, at] * (wgt_ref[:, at] * dep_ref[:, at])
        hi, lo = split(value)
        cell = col_ref[0:1, at]
        pay_ref[0:4, at] = hi
        pay_ref[4:5, at] = lev_ref[:, at].astype(F32)
        pay_ref[5:6, at] = (cell // 256).astype(F32)
        pay_ref[6:7, at] = lax.rem(cell, 256).astype(F32)
        pay_ref[7:8, at] = jnp.ones((1, size), F32)
        pay_ref[8:12, at] = lo
        pay_ref[12:16, at] = jnp.zeros((4, size), F32)
    total = jnp.zeros((tiles * 16, cap), F32)
    step = 512
    for c in range(obs // step):
        at = pl.ds(c * step, step)
        pay = pay_ref[:, at]
        own = own_ref[:, at]
        left = jnp.concatenate(
            [jnp.where(own == t, pay, 0.0).astype(BF16) for t in range(tiles)], axis=0
        )
        right = (rank_ref[:, at] == iota((cap, step), 0)).astype(F32).astype(BF16)
        total = total + dot_nt(left, right)
    for t in range(tiles):
        send_ref[t] = total[t * 16 : t * 16 + 8] + total[t * 16 + 8 : t * 16 + 16]
    pl.semaphore_wait(barrier, tiles - 1)

    def copy_to(k):
        peer = lax.rem(me + k, tiles)
        return pltpu.make_async_remote_copy(
            src_ref=send_ref.at[peer],
            dst_ref=out_ref.at[me],
            send_sem=send_sem.at[k],
            recv_sem=recv_sem.at[k],
            device_id=(ens, peer),
            device_id_type=MESH,
        )

    def start(k, carry):
        copy_to(k).start()
        return carry

    def wait(k, carry):
        copy_to(k).wait()
        return carry

    lax.fori_loop(1, tiles, start, 0)
    out_ref[me] = send_ref[me]
    lax.fori_loop(1, tiles, wait, 0)


def scatter_kernel(recv_ref, vert_ref, out_ref, pos_ref, pay_ref, sort_ref, bound_ref, grad_ref, edge_ref, sem):
    tiles, _, cap = recv_ref.shape
    rows = out_ref.shape[0]
    slots = tiles * cap
    groups = slots // GROUP
    size = min(256, cap)
    per = cap // size
    upper = earlier(size)
    grad_ref[...] = jnp.zeros_like(grad_ref)

    def hot_of(s, c):
        at = pl.ds(c * size, size)
        row, valid = recv_ref[s, 5:6, at], recv_ref[s, 7:8, at]
        key = jnp.where(valid > 0.5, row, -1.0).astype(jnp.int32)
        return (key == iota((rows, size), 0)).astype(F32)

    counts = jnp.zeros((rows, 1), F32)
    for s in range(tiles):
        for c in range(per):
            counts = counts + jnp.sum(hot_of(s, c), axis=1, keepdims=True)
    sub, lane = iota((rows, 128), 0), iota((rows, 128), 1)
    as_row = jnp.sum(jnp.where(sub == lane, counts, 0.0), axis=0, keepdims=True)
    base = jnp.sum(jnp.where(lane < sub, as_row, 0.0), axis=1, keepdims=True)
    start_row = jnp.sum(jnp.where(sub == lane, base, 0.0), axis=0, keepdims=True)
    bound_ref[...] = jnp.concatenate(
        [start_row, start_row + as_row, jnp.zeros((6, 128), F32)], axis=0
    ).astype(jnp.int32)
    bounds = pltpu.make_async_copy(bound_ref, edge_ref, sem)
    bounds.start()
    total = jnp.zeros((groups * 16, GROUP), F32)
    for s in range(tiles):
        for c in range(per):
            at = pl.ds(c * size, size)
            one = hot_of(s, c)
            before = jnp.dot(one.astype(BF16), upper, preferred_element_type=F32)
            pos = jnp.sum(one * (before + base), axis=0, keepdims=True).astype(jnp.int32)
            base = base + jnp.sum(one, axis=1, keepdims=True)
            block = recv_ref[s, :, at]
            hi, lo = split(block)
            pay = jnp.concatenate([hi, lo], axis=0)
            group, place = pos // GROUP, lax.rem(pos, GROUP)
            left = jnp.concatenate(
                [jnp.where(group == g, pay, 0.0).astype(BF16) for g in range(groups)], axis=0
            )
            right = (place == iota((GROUP, size), 0)).astype(F32).astype(BF16)
            total = total + dot_nt(left, right)
    sort_ref[...] = total.reshape(groups, 16, GROUP)
    bounds.wait()

    def one_row(r, carry):
        first, last = edge_ref[0, r], edge_ref[1, r]

        def one_group(g, inner):
            block = sort_ref[g]
            here = block[5:6] == r.astype(F32)
            level = block[4:5].astype(jnp.int32)
            col = block[6:7].astype(jnp.int32)
            hot = (level == iota((128, GROUP), 0)).astype(F32).astype(BF16)
            at0 = col == iota((256, GROUP), 0)
            at1 = jnp.where(col == 255, 0, col + 1) == iota((256, GROUP), 0)
            value = jnp.where(here, block, 0.0)
            for below in range(2):
                part = jnp.zeros((128, 256), F32)
                for low in range(2):
                    k = low * 8 + below * 2
                    mat = jnp.where(
                        at0, value[k : k + 1], jnp.where(at1, value[k + 1 : k + 2], 0.0)
                    ).astype(BF16)
                    part = part + dot_nt(hot, mat)
                grad_ref[r + below] += part
            return inner

        lax.fori_loop(first // GROUP, (last + GROUP - 1) // GROUP, one_group, 0)
        return carry

    lax.fori_loop(0, rows - 1, one_row, 0)
    for x in range(rows):
        out_ref[x] = jnp.dot(vert_ref[...], grad_ref[x], precision=HIGH, preferred_element_type=F32)


def filter_kernel(
    tiles, beta_ref, vert_ref, spread_ref, lan_hbm, prev_hbm, out_hbm, coef_ref,
    lan_ref, prev_ref, halo_ref, spr_ref, diff_ref, sum_ref, all_ref,
    local_sem, halo_send, halo_recv, spr_send, spr_recv, sum_send, sum_recv,
):
    me, ens = lax.axis_index("tile"), lax.axis_index("ens")
    rows, width = spread_ref.shape
    levels = lan_hbm.shape[0] // rows
    wide = SWEEPS
    barrier = greet(tiles, me, ens)
    halves = width // 128
    parts = [pl.ds(h * 128, 128) for h in range(halves)]
    loads = [
        pltpu.make_async_copy(src.at[:, parts[h]], dst.at[h], local_sem.at[i, h])
        for i, (src, dst) in enumerate(((lan_hbm, lan_ref), (prev_hbm, prev_ref)))
        for h in range(halves)
    ]
    for load in loads:
        load.start()
    for side, edge in enumerate((0, tiles - 1)):

        @pl.when(me == edge)
        def _():
            halo_ref[side] = jnp.zeros(halo_ref.shape[1:], F32)
            spr_ref[side] = jnp.zeros(spr_ref.shape[1:], F32)

    pl.semaphore_wait(barrier, tiles - 1)

    def copies(side):
        peer = me + 1 if side == 0 else me - 1
        peer = jnp.clip(peer, 0, tiles - 1)
        begin = rows - wide if side == 0 else 0
        halo = pltpu.make_async_remote_copy(
            src_ref=vert_ref.at[pl.ds(begin, wide)],
            dst_ref=halo_ref.at[side],
            send_sem=halo_send.at[side],
            recv_sem=halo_recv.at[side],
            device_id=(ens, peer),
            device_id_type=MESH,
        )
        spr = pltpu.make_async_remote_copy(
            src_ref=spread_ref,
            dst_ref=spr_ref.at[side],
            send_sem=spr_send.at[side],
            recv_sem=spr_recv.at[side],
            device_id=(ens, peer),
            device_id_type=MESH,
        )
        return spr, halo

    for side in range(2):
        has = me < tiles - 1 if side == 0 else me > 0

        @pl.when(has)
        def _():
            for one in copies(side):
                one.start()

    for load in loads:
        load.wait()
    for side in range(2):
        sends = me < tiles - 1 if side == 0 else me > 0
        gets = me > 0 if side == 0 else me < tiles - 1

        @pl.when(gets)
        def _():
            for one in copies(side):
                one.wait_recv()

        @pl.when(sends)
        def _():
            for one in copies(side):
                one.wait_send()

    beta_prev = beta_ref[0]
    sum_ref[...] = jnp.zeros_like(sum_ref)

    def spread_row(x):
        if x < 0:
            return spr_ref[0, rows + x : rows + x + 1, :]
        if x >= rows:
            return spr_ref[1, x - rows : x - rows + 1, :]
        return spread_ref[x : x + 1, :]

    def strided(ref, begin, count, x):
        where = pl.ds(begin * rows + x, count, stride=rows)
        return jnp.concatenate([ref[h, where, :] for h in range(halves)], axis=1)

    def chunk(begin, count):
        at = pl.ds(begin, count)
        field = {}
        for x in range(-wide, rows + wide):
            if x < 0:
                field[x] = halo_ref[0, wide + x, at, :]
            elif x >= rows:
                field[x] = halo_ref[1, x - rows, at, :]
            else:
                field[x] = vert_ref[x, at, :]
        for sweep in range(SWEEPS):
            reach = wide - sweep
            pushed = {x: spread_row(x) * field[x] for x in range(-reach, rows + reach)}
            for x in range(1 - reach, rows + reach - 1):
                p = pushed[x]
                field[x] = field[x] + (
                    pushed[x + 1] + pushed[x - 1]
                    + pltpu.roll(p, 1, 1) + pltpu.roll(p, width - 1, 1) - 4.0 * p
                )
        dl = jnp.zeros((count, width), F32)
        ll, dd = dl, dl
        for x in range(rows):
            lan = strided(lan_ref, begin, count, x)
            diff = field[x] - beta_prev * strided(prev_ref, begin, count, x)
            diff_ref[x, at, :] = diff
            dl, ll, dd = dl + diff * lan, ll + lan * lan, dd + diff * diff
        for i, value in enumerate((dl, ll, dd)):
            row = jnp.sum(value, axis=0, keepdims=True)
            sum_ref[i : i + 1, :] += row[:, :128] + row[:, 128:]

    full = levels // 8
    pl.loop(0, full)(lambda c: chunk(pl.multiple_of(c * 8, 8), 8))
    if levels % 8:
        chunk(full * 8, levels % 8)

    def share(k):
        peer = lax.rem(me + k, tiles)
        return pltpu.make_async_remote_copy(
            src_ref=sum_ref,
            dst_ref=all_ref.at[me],
            send_sem=sum_send.at[k],
            recv_sem=sum_recv.at[k],
            device_id=(ens, peer),
            device_id_type=MESH,
        )

    def start(k, carry):
        share(k).start()
        return carry

    def wait(k, carry):
        share(k).wait()
        return carry

    lax.fori_loop(1, tiles, start, 0)
    all_ref[me] = sum_ref[...]
    lax.fori_loop(1, tiles, wait, 0)
    sums = jnp.sum(jnp.sum(all_ref[...], axis=0), axis=1, keepdims=True)
    dl, ll, dd = sums[0:1], sums[1:2], sums[2:3]
    extra = dl / ll
    beta = jnp.sqrt(jnp.maximum(dd - extra * dl, 0.0) / ll + 1e-06)
    coef_ref[0] = (1.0 + extra)[0, 0]
    coef_ref[1] = beta[0, 0]
    scale = 1.0 / beta

    def finish(begin, count):
        for x in range(rows):
            where = pl.ds(begin * rows + x, count, stride=rows)
            for h in range(halves):
                diff = diff_ref[x, pl.ds(begin, count), parts[h]]
                prev_ref[h, where, :] = (diff - extra * lan_ref[h, where, :]) * scale

    pl.loop(0, full)(lambda c: finish(pl.multiple_of(c * 8, 8), 8))
    if levels % 8:
        finish(full * 8, levels % 8)
    stores = [
        pltpu.make_async_copy(prev_ref.at[h], out_hbm.at[:, parts[h]], local_sem.at[0, h])
        for h in range(halves)
    ]
    for store in stores:
        store.start()
    for store in stores:
        store.wait()


def per_device(
    departure, obs_weight, owner_id, obs_level, columns, interp_weight, vert_root,
    spread, lanczos, previous, beta_prev,
):
    tiles = lax.axis_size("tile")
    obs = departure.shape[0]
    cap = 2 * obs // tiles
    rows, width = spread.shape
    levels = lanczos.shape[0]
    vmem = pl.BlockSpec(memory_space=pltpu.VMEM)
    smem = pl.BlockSpec(memory_space=pltpu.SMEM)
    hbm = pl.BlockSpec(memory_space=pl.ANY)
    dma = pltpu.SemaphoreType.DMA
    received = pl.pallas_call(
        functools.partial(route_kernel, tiles, cap),
        out_shape=jax.ShapeDtypeStruct((tiles, 8, cap), F32),
        in_specs=[vmem] * 6,
        out_specs=vmem,
        scratch_shapes=[
            pltpu.VMEM((1, obs), jnp.int32),
            pltpu.VMEM((16, obs), F32),
            pltpu.VMEM((tiles, 8, cap), F32),
            dma((tiles,)),
            dma((tiles,)),
        ],
        compiler_params=pltpu.CompilerParams(
            collective_id=0, has_side_effects=True, vmem_limit_bytes=VMEM_LIMIT
        ),
        name="route",
    )(
        departure.reshape(1, obs), obs_weight.reshape(1, obs), owner_id.reshape(1, obs),
        obs_level.reshape(1, obs), columns, interp_weight,
    )
    root = jnp.pad(vert_root.T, ((0, 128 - levels), (0, 128 - levels)))
    vertical = pl.pallas_call(
        scatter_kernel,
        out_shape=jax.ShapeDtypeStruct((rows, 128, width), F32),
        in_specs=[vmem] * 2,
        out_specs=vmem,
        scratch_shapes=[
            pltpu.VMEM((8, 128), jnp.int32),
            pltpu.VMEM((16, GROUP), F32),
            pltpu.VMEM((tiles * cap // GROUP, 16, GROUP), F32),
            pltpu.VMEM((8, 128), jnp.int32),
            pltpu.VMEM((rows, 128, width), F32),
            pltpu.SMEM((8, 128), jnp.int32),
            dma,
        ],
        compiler_params=pltpu.CompilerParams(vmem_limit_bytes=VMEM_LIMIT),
        name="scatter",
    )(received, root)
    flat = (levels * rows, width)
    vector, coefficients = pl.pallas_call(
        functools.partial(filter_kernel, tiles),
        out_shape=(jax.ShapeDtypeStruct(flat, F32), jax.ShapeDtypeStruct((2,), F32)),
        in_specs=[smem, vmem, vmem, hbm, hbm],
        out_specs=(hbm, smem),
        scratch_shapes=[
            pltpu.VMEM((width // 128, levels * rows, 128), F32),
            pltpu.VMEM((width // 128, levels * rows, 128), F32),
            pltpu.VMEM((2, SWEEPS, 128, width), F32),
            pltpu.VMEM((2, rows, width), F32),
            pltpu.VMEM((rows, 128, width), F32),
            pltpu.VMEM((8, 128), F32),
            pltpu.VMEM((tiles, 8, 128), F32),
            dma((2, width // 128)), dma((2,)), dma((2,)), dma((2,)), dma((2,)),
            dma((tiles,)), dma((tiles,)),
        ],
        compiler_params=pltpu.CompilerParams(
            collective_id=1, has_side_effects=True, vmem_limit_bytes=VMEM_LIMIT
        ),
        name="filter",
    )(beta_prev, vertical, spread, lanczos.reshape(flat), previous.reshape(flat))
    return vector.reshape(lanczos.shape), coefficients


def solution(mesh):
    placed = (
        P(("ens", "tile")),
        P(("ens", "tile")),
        P(("ens", "tile"), None),
        P(("ens", "tile")),
        P(None, ("ens", "tile")),
        P(None, ("ens", "tile")),
        P(),
        P("tile", None),
        P(None, ("ens", "tile"), None),
        P(None, ("ens", "tile"), None),
        P("ens"),
    )
    return jax.shard_map(
        per_device,
        mesh=mesh,
        in_specs=placed,
        out_specs=(P(None, ("ens", "tile"), None), P("ens")),
        check_vma=False,
    )
```

```python
import functools

import jax
import jax.numpy as jnp
from jax import lax
from jax.experimental import pallas as pl
from jax.experimental.pallas import tpu as pltpu
from jax.sharding import PartitionSpec as P

SWEEPS = 4
GROUP = 256
WINDOW = 2
F32 = jnp.float32
BF16 = jnp.bfloat16
HIGH = lax.Precision.HIGHEST
MESH = pl.DeviceIdType.MESH
VMEM_LIMIT = 32 * 1024 * 1024
ROUTE_LIMIT = 60 * 1024 * 1024


def iota(shape, axis):
    return lax.broadcasted_iota(jnp.int32, shape, axis)


def dot_nt(a, b):
    return lax.dot_general(a, b, (((1,), (1,)), ((), ())), preferred_element_type=F32)


def split(x):
    hi = x.astype(BF16).astype(F32)
    return hi, x - hi


def earlier(size):
    return (iota((size, size), 0) < iota((size, size), 1)).astype(BF16)


def greet(tiles, me, ens):
    barrier = pltpu.get_barrier_semaphore()

    def signal(k, carry):
        peer = lax.rem(me + k, tiles)
        pl.semaphore_signal(barrier, inc=1, device_id=(ens, peer), device_id_type=MESH)
        return carry

    lax.fori_loop(1, tiles, signal, 0)
    return barrier


def lifted(row, width):
    return jnp.broadcast_to(row, (16, width)).astype(BF16)


def offsets(row, width):
    return (jnp.broadcast_to(row, (16, width)) - iota((16, width), 0).astype(F32)).astype(BF16)


def one_hot(diff, count, value):
    zero = jnp.zeros_like(value)
    return jnp.concatenate(
        [jnp.where(diff == BF16(16 * a), value, zero) for a in range(count // 16)], axis=0
    )


def spread_out(key, pay, count):
    zero = jnp.zeros_like(pay)
    return jnp.concatenate([jnp.where(key == BF16(g), pay, zero) for g in range(count)], axis=0)


def route_kernel(
    tiles, cap, dep_ref, wgt_ref, own_ref, lev_ref, col_ref, itp_ref, out_ref,
    left_ref, right_ref, send_ref, send_sem, recv_sem,
):
    me, ens = lax.axis_index("tile"), lax.axis_index("ens")
    barrier = greet(tiles, me, ens)
    obs = dep_ref.shape[1]
    size = min(256, cap)
    per = cap // size
    upper = earlier(size)
    base = jnp.zeros((tiles, 1), F32)
    ones = jnp.ones((16, size), BF16)
    for c in range(obs // size):
        at = pl.ds(c * size, size)
        own = own_ref[:, at]
        hot = own == iota((tiles, size), 0)
        one = hot.astype(F32)
        before = jnp.dot(one.astype(BF16), upper, preferred_element_type=F32)
        rank = jnp.sum(one * (before + base), axis=0, keepdims=True).astype(jnp.int32)
        base = base + jnp.sum(one, axis=1, keepdims=True)
        value = itp_ref[:, at] * (wgt_ref[:, at] * dep_ref[:, at])
        hi, lo = split(value)
        cell = col_ref[0:1, at]
        pay = jnp.concatenate(
            [
                hi, lev_ref[:, at].astype(F32), (cell // 256).astype(F32),
                lax.rem(cell, 256).astype(F32), jnp.ones((1, size), F32),
                lo, jnp.zeros((4, size), F32),
            ],
            axis=0,
        ).astype(BF16)
        key = lifted((own * per + rank // size).astype(F32), size)
        left_ref[:, at] = spread_out(key, pay, tiles * per)
        right_ref[:, at] = one_hot(offsets(lax.rem(rank, size).astype(F32), size), size, ones)
    total = dot_nt(left_ref[...], right_ref[...])
    for t in range(tiles):
        for h in range(per):
            k = (t * per + h) * 16
            send_ref[t, :, h * size : (h + 1) * size] = total[k : k + 8] + total[k + 8 : k + 16]
    pl.semaphore_wait(barrier, tiles - 1)

    def copy_to(k):
        peer = lax.rem(me + k, tiles)
        return pltpu.make_async_remote_copy(
            src_ref=send_ref.at[peer],
            dst_ref=out_ref.at[me],
            send_sem=send_sem.at[k],
            recv_sem=recv_sem.at[k],
            device_id=(ens, peer),
            device_id_type=MESH,
        )

    def start(k, carry):
        copy_to(k).start()
        return carry

    def wait(k, carry):
        copy_to(k).wait()
        return carry

    lax.fori_loop(1, tiles, start, 0)
    out_ref[me] = send_ref[me]
    lax.fori_loop(1, tiles, wait, 0)


def scatter_kernel(
    recv_ref, root_ref, out_ref, left_ref, right_ref, sort_ref, bound_ref, grad_ref, vert_ref, edge_ref, sem
):
    tiles, _, cap = recv_ref.shape
    rows = out_ref.shape[0]
    levels = root_ref.shape[0]
    slots = tiles * cap
    groups = slots // GROUP
    size = min(256, cap)
    per = cap // size
    upper = earlier(size)
    grad_ref[...] = jnp.zeros_like(grad_ref)
    vert_ref[...] = jnp.zeros_like(vert_ref)
    vert_ref[:levels, :levels] = root_ref[...]
    root = vert_ref[...].T
    ones = jnp.ones((16, GROUP), BF16)

    def hot_of(s, c):
        at = pl.ds(c * size, size)
        row, valid = recv_ref[s, 5:6, at], recv_ref[s, 7:8, at]
        key = jnp.where(valid > 0.5, row, -1.0).astype(jnp.int32)
        return (key == iota((rows, size), 0)).astype(F32)

    counts = jnp.zeros((rows, 1), F32)
    for s in range(tiles):
        for c in range(per):
            counts = counts + jnp.sum(hot_of(s, c), axis=1, keepdims=True)
    sub, lane = iota((rows, 128), 0), iota((rows, 128), 1)
    as_row = jnp.sum(jnp.where(sub == lane, counts, 0.0), axis=0, keepdims=True)
    base = jnp.sum(jnp.where(lane < sub, as_row, 0.0), axis=1, keepdims=True)
    start_row = jnp.sum(jnp.where(sub == lane, base, 0.0), axis=0, keepdims=True)
    bound_ref[...] = jnp.concatenate(
        [start_row, start_row + as_row, jnp.zeros((6, 128), F32)], axis=0
    ).astype(jnp.int32)
    bounds = pltpu.make_async_copy(bound_ref, edge_ref, sem)
    bounds.start()
    for s in range(tiles):
        for c in range(per):
            at = pl.ds(c * size, size)
            to = pl.ds((s * per + c) * size, size)
            one = hot_of(s, c)
            before = jnp.dot(one.astype(BF16), upper, preferred_element_type=F32)
            pos = jnp.sum(one * (before + base), axis=0, keepdims=True).astype(jnp.int32)
            base = base + jnp.sum(one, axis=1, keepdims=True)
            hi, lo = split(recv_ref[s, :, at])
            pay = jnp.concatenate([hi, lo], axis=0).astype(BF16)
            left_ref[:, to] = spread_out(lifted((pos // GROUP).astype(F32), size), pay, groups)
            right_ref[:, to] = one_hot(
                offsets(lax.rem(pos, GROUP).astype(F32), size), GROUP, ones[:, :size]
            )
    total = dot_nt(left_ref[...], right_ref[...])
    sort_ref[:groups] = total.reshape(groups, 16, GROUP)
    for w in range(groups, sort_ref.shape[0]):
        sort_ref[w] = jnp.zeros((16, GROUP), F32)
    bounds.wait()

    def one_row(r, carry):
        first, last = edge_ref[0, r], edge_ref[1, r]
        begin = first // GROUP
        end = jnp.where(last > first, (last + GROUP - 1) // GROUP, begin)

        def window(i, inner):
            hots, lefts = [], []
            for w in range(WINDOW):
                block = sort_ref[begin + i * WINDOW + w]
                value = jnp.where(block[5:6] == r.astype(F32), block, 0.0)
                hots.append(one_hot(offsets(block[6:7], GROUP), 256, ones))
                diff = offsets(block[4:5], GROUP)
                for low in (0, 8):
                    lefts.append(jnp.concatenate(
                        [one_hot(diff, 128, lifted(value[low + k : low + k + 1], GROUP)) for k in range(4)],
                        axis=0,
                    ))
            right = jnp.concatenate([h for h in hots for low in range(2)], axis=1)
            part = dot_nt(jnp.concatenate(lefts, axis=1), right)
            for k in range(4):
                grad_ref[k % 2, r + k // 2] += part[k * 128 : (k + 1) * 128]
            return inner

        lax.fori_loop(0, (end - begin + WINDOW - 1) // WINDOW, window, 0)
        return carry

    lax.fori_loop(0, rows - 1, one_row, 0)
    for x in range(rows):
        grad = grad_ref[0, x] + pltpu.roll(grad_ref[1, x], 1, 1)
        out_ref[x] = jnp.dot(root, grad, precision=HIGH, preferred_element_type=F32)


def filter_kernel(
    tiles, beta_ref, vert_ref, spread_ref, lan_hbm, prev_hbm, out_hbm, coef_ref,
    lan_ref, prev_ref, halo_ref, spr_ref, diff_ref, sum_ref, all_ref,
    local_sem, halo_send, halo_recv, spr_send, spr_recv, sum_send, sum_recv,
):
    me, ens = lax.axis_index("tile"), lax.axis_index("ens")
    rows, width = spread_ref.shape
    levels = lan_hbm.shape[0] // rows
    wide = SWEEPS
    barrier = greet(tiles, me, ens)
    halves = width // 128
    parts = [pl.ds(h * 128, 128) for h in range(halves)]
    loads = [
        pltpu.make_async_copy(src.at[:, parts[h]], dst.at[h], local_sem.at[i, h])
        for i, (src, dst) in enumerate(((lan_hbm, lan_ref), (prev_hbm, prev_ref)))
        for h in range(halves)
    ]
    for load in loads:
        load.start()
    for side, edge in enumerate((0, tiles - 1)):

        @pl.when(me == edge)
        def _():
            halo_ref[side] = jnp.zeros(halo_ref.shape[1:], F32)
            spr_ref[side] = jnp.zeros(spr_ref.shape[1:], F32)

    pl.semaphore_wait(barrier, tiles - 1)

    def copies(side):
        peer = me + 1 if side == 0 else me - 1
        peer = jnp.clip(peer, 0, tiles - 1)
        begin = rows - wide if side == 0 else 0
        halo = pltpu.make_async_remote_copy(
            src_ref=vert_ref.at[pl.ds(begin, wide)],
            dst_ref=halo_ref.at[side],
            send_sem=halo_send.at[side],
            recv_sem=halo_recv.at[side],
            device_id=(ens, peer),
            device_id_type=MESH,
        )
        spr = pltpu.make_async_remote_copy(
            src_ref=spread_ref,
            dst_ref=spr_ref.at[side],
            send_sem=spr_send.at[side],
            recv_sem=spr_recv.at[side],
            device_id=(ens, peer),
            device_id_type=MESH,
        )
        return spr, halo

    for side in range(2):
        has = me < tiles - 1 if side == 0 else me > 0

        @pl.when(has)
        def _():
            for one in copies(side):
                one.start()

    for load in loads:
        load.wait()
    for side in range(2):
        sends = me < tiles - 1 if side == 0 else me > 0
        gets = me > 0 if side == 0 else me < tiles - 1

        @pl.when(gets)
        def _():
            for one in copies(side):
                one.wait_recv()

        @pl.when(sends)
        def _():
            for one in copies(side):
                one.wait_send()

    beta_prev = beta_ref[0]
    sum_ref[...] = jnp.zeros_like(sum_ref)

    def spread_row(x):
        if x < 0:
            return spr_ref[0, rows + x : rows + x + 1, :]
        if x >= rows:
            return spr_ref[1, x - rows : x - rows + 1, :]
        return spread_ref[x : x + 1, :]

    def strided(ref, begin, count, x):
        where = pl.ds(begin * rows + x, count, stride=rows)
        return jnp.concatenate([ref[h, where, :] for h in range(halves)], axis=1)

    def chunk(begin, count):
        at = pl.ds(begin, count)
        field = {}
        for x in range(-wide, rows + wide):
            if x < 0:
                field[x] = halo_ref[0, wide + x, at, :]
            elif x >= rows:
                field[x] = halo_ref[1, x - rows, at, :]
            else:
                field[x] = vert_ref[x, at, :]
        for sweep in range(SWEEPS):
            reach = wide - sweep
            pushed = {x: spread_row(x) * field[x] for x in range(-reach, rows + reach)}
            for x in range(1 - reach, rows + reach - 1):
                p = pushed[x]
                field[x] = field[x] + (
                    pushed[x + 1] + pushed[x - 1]
                    + pltpu.roll(p, 1, 1) + pltpu.roll(p, width - 1, 1) - 4.0 * p
                )
        dl = jnp.zeros((count, width), F32)
        ll, dd = dl, dl
        for x in range(rows):
            lan = strided(lan_ref, begin, count, x)
            diff = field[x] - beta_prev * strided(prev_ref, begin, count, x)
            diff_ref[x, at, :] = diff
            dl, ll, dd = dl + diff * lan, ll + lan * lan, dd + diff * diff
        for i, value in enumerate((dl, ll, dd)):
            row = jnp.sum(value, axis=0, keepdims=True)
            sum_ref[i : i + 1, :] += row[:, :128] + row[:, 128:]

    full = levels // 8
    pl.loop(0, full)(lambda c: chunk(pl.multiple_of(c * 8, 8), 8))
    if levels % 8:
        chunk(full * 8, levels % 8)

    def share(k):
        peer = lax.rem(me + k, tiles)
        return pltpu.make_async_remote_copy(
            src_ref=sum_ref,
            dst_ref=all_ref.at[me],
            send_sem=sum_send.at[k],
            recv_sem=sum_recv.at[k],
            device_id=(ens, peer),
            device_id_type=MESH,
        )

    def start(k, carry):
        share(k).start()
        return carry

    def wait(k, carry):
        share(k).wait()
        return carry

    lax.fori_loop(1, tiles, start, 0)
    all_ref[me] = sum_ref[...]
    lax.fori_loop(1, tiles, wait, 0)
    sums = jnp.sum(jnp.sum(all_ref[...], axis=0), axis=1, keepdims=True)
    dl, ll, dd = sums[0:1], sums[1:2], sums[2:3]
    extra = dl / ll
    beta = jnp.sqrt(jnp.maximum(dd - extra * dl, 0.0) / ll + 1e-06)
    coef_ref[0] = (1.0 + extra)[0, 0]
    coef_ref[1] = beta[0, 0]
    scale = 1.0 / beta

    def finish(begin, count):
        for x in range(rows):
            where = pl.ds(begin * rows + x, count, stride=rows)
            for h in range(halves):
                diff = diff_ref[x, pl.ds(begin, count), parts[h]]
                prev_ref[h, where, :] = (diff - extra * lan_ref[h, where, :]) * scale

    pl.loop(0, full)(lambda c: finish(pl.multiple_of(c * 8, 8), 8))
    if levels % 8:
        finish(full * 8, levels % 8)
    stores = [
        pltpu.make_async_copy(prev_ref.at[h], out_hbm.at[:, parts[h]], local_sem.at[0, h])
        for h in range(halves)
    ]
    for store in stores:
        store.start()
    for store in stores:
        store.wait()


def per_device(
    departure, obs_weight, owner_id, obs_level, columns, interp_weight, vert_root,
    spread, lanczos, previous, beta_prev,
):
    tiles = lax.axis_size("tile")
    obs = departure.shape[0]
    cap = 2 * obs // tiles
    rows, width = spread.shape
    levels = lanczos.shape[0]
    size = min(256, cap)
    slots = tiles * cap
    vmem = pl.BlockSpec(memory_space=pltpu.VMEM)
    smem = pl.BlockSpec(memory_space=pltpu.SMEM)
    hbm = pl.BlockSpec(memory_space=pl.ANY)
    dma = pltpu.SemaphoreType.DMA
    received = pl.pallas_call(
        functools.partial(route_kernel, tiles, cap),
        out_shape=jax.ShapeDtypeStruct((tiles, 8, cap), F32),
        in_specs=[vmem] * 6,
        out_specs=vmem,
        scratch_shapes=[
            pltpu.VMEM((tiles * cap // size * 16, obs), BF16),
            pltpu.VMEM((size, obs), BF16),
            pltpu.VMEM((tiles, 8, cap), F32),
            dma((tiles,)),
            dma((tiles,)),
        ],
        compiler_params=pltpu.CompilerParams(
            collective_id=0, has_side_effects=True, vmem_limit_bytes=ROUTE_LIMIT
        ),
        name="route",
    )(
        departure.reshape(1, obs), obs_weight.reshape(1, obs), owner_id.reshape(1, obs),
        obs_level.reshape(1, obs), columns, interp_weight,
    )
    vertical = pl.pallas_call(
        scatter_kernel,
        out_shape=jax.ShapeDtypeStruct((rows, 128, width), F32),
        in_specs=[vmem] * 2,
        out_specs=vmem,
        scratch_shapes=[
            pltpu.VMEM((slots // GROUP * 16, slots), BF16),
            pltpu.VMEM((GROUP, slots), BF16),
            pltpu.VMEM((slots // GROUP + WINDOW - 1, 16, GROUP), F32),
            pltpu.VMEM((8, 128), jnp.int32),
            pltpu.VMEM((2, rows, 128, width), F32),
            pltpu.VMEM((128, 128), F32),
            pltpu.SMEM((8, 128), jnp.int32),
            dma,
        ],
        compiler_params=pltpu.CompilerParams(vmem_limit_bytes=VMEM_LIMIT),
        name="scatter",
    )(received, vert_root)
    flat = (levels * rows, width)
    vector, coefficients = pl.pallas_call(
        functools.partial(filter_kernel, tiles),
        out_shape=(jax.ShapeDtypeStruct(flat, F32), jax.ShapeDtypeStruct((2,), F32)),
        in_specs=[smem, vmem, vmem, hbm, hbm],
        out_specs=(hbm, smem),
        scratch_shapes=[
            pltpu.VMEM((width // 128, levels * rows, 128), F32),
            pltpu.VMEM((width // 128, levels * rows, 128), F32),
            pltpu.VMEM((2, SWEEPS, 128, width), F32),
            pltpu.VMEM((2, rows, width), F32),
            pltpu.VMEM((rows, 128, width), F32),
            pltpu.VMEM((8, 128), F32),
            pltpu.VMEM((tiles, 8, 128), F32),
            dma((2, width // 128)), dma((2,)), dma((2,)), dma((2,)), dma((2,)),
            dma((tiles,)), dma((tiles,)),
        ],
        compiler_params=pltpu.CompilerParams(
            collective_id=1, has_side_effects=True, vmem_limit_bytes=VMEM_LIMIT
        ),
        name="filter",
    )(beta_prev, vertical, spread, lanczos.reshape(flat), previous.reshape(flat))
    return vector.reshape(lanczos.shape), coefficients


def solution(mesh):
    placed = (
        P(("ens", "tile")),
        P(("ens", "tile")),
        P(("ens", "tile"), None),
        P(("ens", "tile")),
        P(None, ("ens", "tile")),
        P(None, ("ens", "tile")),
        P(),
        P("tile", None),
        P(None, ("ens", "tile"), None),
        P(None, ("ens", "tile"), None),
        P("ens"),
    )
    return jax.shard_map(
        per_device,
        mesh=mesh,
        in_specs=placed,
        out_specs=(P(None, ("ens", "tile"), None), P("ens")),
        check_vma=False,
    )
```

```python
import functools

import jax
import jax.numpy as jnp
from jax import lax
from jax.experimental import pallas as pl
from jax.experimental.pallas import tpu as pltpu
from jax.sharding import PartitionSpec as P

SWEEPS = 4
GROUP = 256
WINDOW = 2
F32 = jnp.float32
BF16 = jnp.bfloat16
HIGH = lax.Precision.HIGHEST
MESH = pl.DeviceIdType.MESH
VMEM_LIMIT = 32 * 1024 * 1024
ROUTE_LIMIT = 60 * 1024 * 1024


def iota(shape, axis):
    return lax.broadcasted_iota(jnp.int32, shape, axis)


def dot_nt(a, b):
    return lax.dot_general(a, b, (((1,), (1,)), ((), ())), preferred_element_type=F32)


def split(x):
    hi = x.astype(BF16).astype(F32)
    return hi, x - hi


def earlier(size):
    return (iota((size, size), 0) < iota((size, size), 1)).astype(BF16)


def greet(tiles, me, ens):
    barrier = pltpu.get_barrier_semaphore()

    def signal(k, carry):
        peer = lax.rem(me + k, tiles)
        pl.semaphore_signal(barrier, inc=1, device_id=(ens, peer), device_id_type=MESH)
        return carry

    lax.fori_loop(1, tiles, signal, 0)
    return barrier


def lifted(row, width):
    return jnp.broadcast_to(row, (16, width)).astype(BF16)


def offsets(row, width):
    return (jnp.broadcast_to(row, (16, width)) - iota((16, width), 0).astype(F32)).astype(BF16)


def one_hot(diff, count, value):
    zero = jnp.zeros_like(value)
    return jnp.concatenate(
        [jnp.where(diff == BF16(16 * a), value, zero) for a in range(count // 16)], axis=0
    )


def spread_out(key, pay, count):
    zero = jnp.zeros_like(pay)
    return jnp.concatenate([jnp.where(key == BF16(g), pay, zero) for g in range(count)], axis=0)


def route_kernel(
    tiles, cap, dep_ref, wgt_ref, own_ref, lev_ref, col_ref, itp_ref, spread_ref, out_ref, spr_ref,
    left_ref, right_ref, send_ref, send_sem, recv_sem, spr_send, spr_recv,
):
    me, ens = lax.axis_index("tile"), lax.axis_index("ens")
    barrier = greet(tiles, me, ens)
    obs = dep_ref.shape[1]
    size = min(256, cap)
    per = cap // size
    upper = earlier(size)
    base = jnp.zeros((tiles, 1), F32)
    ones = jnp.ones((16, size), BF16)
    for c in range(obs // size):
        at = pl.ds(c * size, size)
        own = own_ref[:, at]
        hot = own == iota((tiles, size), 0)
        one = hot.astype(F32)
        before = jnp.dot(one.astype(BF16), upper, preferred_element_type=F32)
        rank = jnp.sum(one * (before + base), axis=0, keepdims=True).astype(jnp.int32)
        base = base + jnp.sum(one, axis=1, keepdims=True)
        value = itp_ref[:, at] * (wgt_ref[:, at] * dep_ref[:, at])
        hi, lo = split(value)
        cell = col_ref[0:1, at]
        pay = jnp.concatenate(
            [
                hi, lev_ref[:, at].astype(F32), (cell // 256).astype(F32),
                lax.rem(cell, 256).astype(F32), jnp.ones((1, size), F32),
                lo, jnp.zeros((4, size), F32),
            ],
            axis=0,
        ).astype(BF16)
        key = lifted((own * per + rank // size).astype(F32), size)
        left_ref[:, at] = spread_out(key, pay, tiles * per)
        right_ref[:, at] = one_hot(offsets(lax.rem(rank, size).astype(F32), size), size, ones)
    total = dot_nt(left_ref[...], right_ref[...])
    for t in range(tiles):
        for h in range(per):
            k = (t * per + h) * 16
            send_ref[t, :, h * size : (h + 1) * size] = total[k : k + 8] + total[k + 8 : k + 16]
    for side, edge in enumerate((0, tiles - 1)):

        @pl.when(me == edge)
        def _():
            spr_ref[side] = jnp.zeros(spr_ref.shape[1:], F32)

    pl.semaphore_wait(barrier, tiles - 1)

    def spr_copy(side):
        peer = jnp.clip(me + 1 if side == 0 else me - 1, 0, tiles - 1)
        return pltpu.make_async_remote_copy(
            src_ref=spread_ref,
            dst_ref=spr_ref.at[side],
            send_sem=spr_send.at[side],
            recv_sem=spr_recv.at[side],
            device_id=(ens, peer),
            device_id_type=MESH,
        )

    def copy_to(k):
        peer = lax.rem(me + k, tiles)
        return pltpu.make_async_remote_copy(
            src_ref=send_ref.at[peer],
            dst_ref=out_ref.at[me],
            send_sem=send_sem.at[k],
            recv_sem=recv_sem.at[k],
            device_id=(ens, peer),
            device_id_type=MESH,
        )

    def start(k, carry):
        copy_to(k).start()
        return carry

    def wait(k, carry):
        copy_to(k).wait()
        return carry

    lax.fori_loop(1, tiles, start, 0)
    sends = (me < tiles - 1, me > 0)
    for side in range(2):
        pl.when(sends[side])(spr_copy(side).start)
    out_ref[me] = send_ref[me]
    lax.fori_loop(1, tiles, wait, 0)
    for side in range(2):
        pl.when(sends[1 - side])(spr_copy(side).wait_recv)
        pl.when(sends[side])(spr_copy(side).wait_send)


def load_root(root_ref, vert_ref):
    levels = root_ref.shape[0]
    vert_ref[...] = jnp.zeros_like(vert_ref)
    vert_ref[:levels, :levels] = root_ref[...]
    return vert_ref[...].T


def add_rows(low, high, edge_ref, sort_ref, grad_ref):
    ones = jnp.ones((16, GROUP), BF16)

    def one_row(r, carry):
        first, last = edge_ref[0, r], edge_ref[1, r]
        begin = first // GROUP
        end = jnp.where(last > first, (last + GROUP - 1) // GROUP, begin)

        def window(i, inner):
            hots, lefts = [], []
            for w in range(WINDOW):
                block = sort_ref[begin + i * WINDOW + w]
                value = jnp.where(block[5:6] == r.astype(F32), block, 0.0)
                hots.append(one_hot(offsets(block[6:7], GROUP), 256, ones))
                diff = offsets(block[4:5], GROUP)
                for low in (0, 8):
                    lefts.append(jnp.concatenate(
                        [one_hot(diff, 128, lifted(value[low + k : low + k + 1], GROUP)) for k in range(4)],
                        axis=0,
                    ))
            right = jnp.concatenate([h for h in hots for low in range(2)], axis=1)
            part = dot_nt(jnp.concatenate(lefts, axis=1), right)
            for k in range(4):
                grad_ref[k % 2, r + k // 2] += part[k * 128 : (k + 1) * 128]
            return inner

        lax.fori_loop(0, (end - begin + WINDOW - 1) // WINDOW, window, 0)
        return carry

    lax.fori_loop(low, high, one_row, 0)


def levels_of(root, grad_ref, x):
    grad = grad_ref[0, x] + pltpu.roll(grad_ref[1, x], 1, 1)
    return jnp.dot(root, grad, precision=HIGH, preferred_element_type=F32)


def scatter_kernel(
    recv_ref, root_ref, low_ref, high_ref, sort_ref, bound_ref, part_ref,
    left_ref, right_ref, grad_ref, vert_ref, edge_ref, sem,
):
    tiles, _, cap = recv_ref.shape
    rows = grad_ref.shape[1]
    wide = SWEEPS
    slots = tiles * cap
    groups = slots // GROUP
    size = min(256, cap)
    per = cap // size
    upper = earlier(size)
    grad_ref[...] = jnp.zeros_like(grad_ref)
    root = load_root(root_ref, vert_ref)
    ones = jnp.ones((16, GROUP), BF16)

    def hot_of(s, c):
        at = pl.ds(c * size, size)
        row, valid = recv_ref[s, 5:6, at], recv_ref[s, 7:8, at]
        key = jnp.where(valid > 0.5, row, -1.0).astype(jnp.int32)
        return (key == iota((rows, size), 0)).astype(F32)

    counts = jnp.zeros((rows, 1), F32)
    for s in range(tiles):
        for c in range(per):
            counts = counts + jnp.sum(hot_of(s, c), axis=1, keepdims=True)
    sub, lane = iota((rows, 128), 0), iota((rows, 128), 1)
    as_row = jnp.sum(jnp.where(sub == lane, counts, 0.0), axis=0, keepdims=True)
    base = jnp.sum(jnp.where(lane < sub, as_row, 0.0), axis=1, keepdims=True)
    start_row = jnp.sum(jnp.where(sub == lane, base, 0.0), axis=0, keepdims=True)
    bound_ref[...] = jnp.concatenate(
        [start_row, start_row + as_row, jnp.zeros((6, 128), F32)], axis=0
    ).astype(jnp.int32)
    bounds = pltpu.make_async_copy(bound_ref, edge_ref, sem)
    bounds.start()
    for s in range(tiles):
        for c in range(per):
            at = pl.ds(c * size, size)
            to = pl.ds((s * per + c) * size, size)
            one = hot_of(s, c)
            before = jnp.dot(one.astype(BF16), upper, preferred_element_type=F32)
            pos = jnp.sum(one * (before + base), axis=0, keepdims=True).astype(jnp.int32)
            base = base + jnp.sum(one, axis=1, keepdims=True)
            hi, lo = split(recv_ref[s, :, at])
            pay = jnp.concatenate([hi, lo], axis=0).astype(BF16)
            left_ref[:, to] = spread_out(lifted((pos // GROUP).astype(F32), size), pay, groups)
            right_ref[:, to] = one_hot(
                offsets(lax.rem(pos, GROUP).astype(F32), size), GROUP, ones[:, :size]
            )
    total = dot_nt(left_ref[...], right_ref[...])
    sort_ref[:groups] = total.reshape(groups, 16, GROUP)
    for w in range(groups, sort_ref.shape[0]):
        sort_ref[w] = jnp.zeros((16, GROUP), F32)
    bounds.wait()

    add_rows(0, wide, edge_ref, sort_ref, grad_ref)
    add_rows(rows - wide - 1, rows - 1, edge_ref, sort_ref, grad_ref)
    for x in range(wide):
        low_ref[x] = levels_of(root, grad_ref, x)
        high_ref[x] = levels_of(root, grad_ref, rows - wide + x)
    for dj in range(2):
        part_ref[0, dj] = grad_ref[dj, wide]
        part_ref[1, dj] = grad_ref[dj, rows - wide - 1]


def sweep_rows(field, spread_of, low, high):
    width = field[low].shape[1]
    for sweep in range(SWEEPS):
        pushed = {x: spread_of(x) * field[x] for x in range(low, high)}
        low, high = low + 1, high - 1
        for x in range(low, high):
            p = pushed[x]
            field[x] = field[x] + (
                pushed[x + 1] + pushed[x - 1]
                + pltpu.roll(p, 1, 1) + pltpu.roll(p, width - 1, 1) - 4.0 * p
            )
    return field


def strided(ref, begin, count, x, rows):
    where = pl.ds(begin * rows + x, count, stride=rows)
    return jnp.concatenate([ref[h, where, :] for h in range(ref.shape[0])], axis=1)


def add_sums(sum_ref, pairs):
    dl, ll, dd = (sum(v) for v in zip(*[(d * l, l * l, d * d) for d, l in pairs]))
    for i, value in enumerate((dl, ll, dd)):
        row = jnp.sum(value, axis=0, keepdims=True)
        sum_ref[i : i + 1, :] += row[:, :128] + row[:, 128:]


def for_levels(levels, chunk):
    full = levels // 8
    pl.loop(0, full)(lambda c: chunk(pl.multiple_of(c * 8, 8), 8))
    if levels % 8:
        chunk(full * 8, levels % 8)


def loads_of(pairs, sem):
    return [
        pltpu.make_async_copy(src.at[:, pl.ds(h * 128, 128)], dst.at[h], sem.at[i, h])
        for i, (src, dst) in enumerate(pairs)
        for h in range(dst.shape[0])
    ]


def inner_kernel(
    beta_ref, low_ref, high_ref, sort_ref, bound_ref, part_ref, root_ref, spread_ref, lan_hbm, prev_hbm,
    mid_ref, diff_ref, sum_ref, grad_ref, vert_ref, edge_ref, lan_ref, prev_ref, sem, local_sem,
):
    rows = spread_ref.shape[0]
    levels = root_ref.shape[0]
    wide = SWEEPS
    bounds = pltpu.make_async_copy(bound_ref, edge_ref, sem)
    bounds.start()
    loads = loads_of(((lan_hbm, lan_ref), (prev_hbm, prev_ref)), local_sem)
    for load in loads:
        load.start()
    for dj in range(2):
        grad_ref[dj, wide] = part_ref[0, dj]
        grad_ref[dj, rows - wide - 1] = part_ref[1, dj]
        for x in range(wide + 1, rows - wide - 1):
            grad_ref[dj, x] = jnp.zeros(grad_ref.shape[2:], F32)
    root = load_root(root_ref, vert_ref)
    bounds.wait()
    add_rows(wide, rows - wide - 1, edge_ref, sort_ref, grad_ref)
    for x in range(wide, rows - wide):
        mid_ref[x - wide] = levels_of(root, grad_ref, x)
    for load in loads:
        load.wait()
    beta_prev = beta_ref[0]
    sum_ref[...] = jnp.zeros_like(sum_ref)

    def chunk(begin, count):
        at = pl.ds(begin, count)
        field = {x: low_ref[x, at, :] for x in range(wide)}
        field.update({x: mid_ref[x - wide, at, :] for x in range(wide, rows - wide)})
        field.update({x: high_ref[x - rows + wide, at, :] for x in range(rows - wide, rows)})
        field = sweep_rows(field, lambda x: spread_ref[x : x + 1, :], 0, rows)
        pairs = []
        for x in range(wide, rows - wide):
            diff = field[x] - beta_prev * strided(prev_ref, begin, count, x, rows)
            diff_ref[x - wide, at, :] = diff
            pairs.append((diff, strided(lan_ref, begin, count, x, rows)))
        add_sums(sum_ref, pairs)

    for_levels(levels, chunk)


def filter_kernel(
    tiles, beta_ref, low_ref, mid_ref, high_ref, below_ref, above_ref, inner_ref, part_ref, spread_ref, spr_ref,
    lan_hbm, prev_hbm, out_hbm, coef_ref,
    lan_ref, prev_ref, diff_ref, sum_ref, all_ref, local_sem, sum_send, sum_recv,
):
    me, ens = lax.axis_index("tile"), lax.axis_index("ens")
    rows, width = spread_ref.shape
    levels = lan_hbm.shape[0] // rows
    wide = SWEEPS
    barrier = greet(tiles, me, ens)
    loads = loads_of(((lan_hbm, lan_ref), (prev_hbm, prev_ref)), local_sem)
    for load in loads:
        load.start()
    for load in loads:
        load.wait()
    beta_prev = beta_ref[0]
    sum_ref[...] = part_ref[...]

    def spread_row(x):
        if x < 0:
            return spr_ref[0, rows + x : rows + x + 1, :]
        if x >= rows:
            return spr_ref[1, x - rows : x - rows + 1, :]
        return spread_ref[x : x + 1, :]

    def field_row(x, at):
        for ref, begin in ((below_ref, -wide), (low_ref, 0), (mid_ref, wide), (high_ref, rows - wide), (above_ref, rows)):
            if begin <= x < begin + ref.shape[0]:
                return ref[x - begin, at, :]

    def chunk(begin, count):
        at = pl.ds(begin, count)
        pairs = []
        for first in (0, rows - wide):
            span = (first - wide, first + 2 * wide)
            field = sweep_rows({x: field_row(x, at) for x in range(*span)}, spread_row, *span)
            for x in range(first, first + wide):
                diff = field[x] - beta_prev * strided(prev_ref, begin, count, x, rows)
                diff_ref[x % (2 * wide), at, :] = diff
                pairs.append((diff, strided(lan_ref, begin, count, x, rows)))
        add_sums(sum_ref, pairs)

    for_levels(levels, chunk)
    pl.semaphore_wait(barrier, tiles - 1)

    def share(k):
        peer = lax.rem(me + k, tiles)
        return pltpu.make_async_remote_copy(
            src_ref=sum_ref,
            dst_ref=all_ref.at[me],
            send_sem=sum_send.at[k],
            recv_sem=sum_recv.at[k],
            device_id=(ens, peer),
            device_id_type=MESH,
        )

    def start(k, carry):
        share(k).start()
        return carry

    def wait(k, carry):
        share(k).wait()
        return carry

    lax.fori_loop(1, tiles, start, 0)
    all_ref[me] = sum_ref[...]
    lax.fori_loop(1, tiles, wait, 0)
    sums = jnp.sum(jnp.sum(all_ref[...], axis=0), axis=1, keepdims=True)
    dl, ll, dd = sums[0:1], sums[1:2], sums[2:3]
    extra = dl / ll
    beta = jnp.sqrt(jnp.maximum(dd - extra * dl, 0.0) / ll + 1e-06)
    coef_ref[0] = (1.0 + extra)[0, 0]
    coef_ref[1] = beta[0, 0]
    scale = 1.0 / beta

    def finish(begin, count):
        for x in range(rows):
            where = pl.ds(begin * rows + x, count, stride=rows)
            for h in range(width // 128):
                at = (pl.ds(begin, count), pl.ds(h * 128, 128))
                if wide <= x < rows - wide:
                    diff = inner_ref[x - wide, *at]
                else:
                    diff = diff_ref[x % (2 * wide), *at]
                prev_ref[h, where, :] = (diff - extra * lan_ref[h, where, :]) * scale

    for_levels(levels, finish)
    stores = [
        pltpu.make_async_copy(prev_ref.at[h], out_hbm.at[:, pl.ds(h * 128, 128)], local_sem.at[0, h])
        for h in range(width // 128)
    ]
    for store in stores:
        store.start()
    for store in stores:
        store.wait()


def per_device(
    departure, obs_weight, owner_id, obs_level, columns, interp_weight, vert_root,
    spread, lanczos, previous, beta_prev,
):
    tiles = lax.axis_size("tile")
    obs = departure.shape[0]
    cap = 2 * obs // tiles
    rows, width = spread.shape
    levels = lanczos.shape[0]
    size = min(256, cap)
    slots = tiles * cap
    vmem = pl.BlockSpec(memory_space=pltpu.VMEM)
    smem = pl.BlockSpec(memory_space=pltpu.SMEM)
    hbm = pl.BlockSpec(memory_space=pl.ANY)
    dma = pltpu.SemaphoreType.DMA
    received, spread_halo = pl.pallas_call(
        functools.partial(route_kernel, tiles, cap),
        out_shape=(
            jax.ShapeDtypeStruct((tiles, 8, cap), F32),
            jax.ShapeDtypeStruct((2, rows, width), F32),
        ),
        in_specs=[vmem] * 7,
        out_specs=(vmem, vmem),
        scratch_shapes=[
            pltpu.VMEM((tiles * cap // size * 16, obs), BF16),
            pltpu.VMEM((size, obs), BF16),
            pltpu.VMEM((tiles, 8, cap), F32),
            dma((tiles,)), dma((tiles,)), dma((2,)), dma((2,)),
        ],
        compiler_params=pltpu.CompilerParams(
            collective_id=0, has_side_effects=True, vmem_limit_bytes=ROUTE_LIMIT
        ),
        name="route",
    )(
        departure.reshape(1, obs), obs_weight.reshape(1, obs), owner_id.reshape(1, obs),
        obs_level.reshape(1, obs), columns, interp_weight, spread,
    )
    flat = (levels * rows, width)
    lan, prev = lanczos.reshape(flat), previous.reshape(flat)
    edge = jax.ShapeDtypeStruct((SWEEPS, 128, width), F32)
    middle = jax.ShapeDtypeStruct((rows - 2 * SWEEPS, 128, width), F32)
    low, high, order, bound, part = pl.pallas_call(
        scatter_kernel,
        out_shape=(
            edge,
            edge,
            jax.ShapeDtypeStruct((slots // GROUP + WINDOW - 1, 16, GROUP), F32),
            jax.ShapeDtypeStruct((8, 128), jnp.int32),
            jax.ShapeDtypeStruct((2, 2, 128, width), F32),
        ),
        in_specs=[vmem] * 2,
        out_specs=[vmem] * 5,
        scratch_shapes=[
            pltpu.VMEM((slots // GROUP * 16, slots), BF16),
            pltpu.VMEM((GROUP, slots), BF16),
            pltpu.VMEM((2, rows, 128, width), F32),
            pltpu.VMEM((128, 128), F32),
            pltpu.SMEM((8, 128), jnp.int32),
            dma,
        ],
        compiler_params=pltpu.CompilerParams(vmem_limit_bytes=VMEM_LIMIT),
        name="scatter",
    )(received, vert_root)
    up = [(i, i + 1) for i in range(tiles - 1)]
    below = lax.ppermute(high, "tile", up)
    above = lax.ppermute(low, "tile", [(j, i) for i, j in up])
    mid, inner, sums = pl.pallas_call(
        inner_kernel,
        out_shape=(middle, middle, jax.ShapeDtypeStruct((8, 128), F32)),
        in_specs=[smem] + [vmem] * 7 + [hbm] * 2,
        out_specs=[vmem] * 3,
        scratch_shapes=[
            pltpu.VMEM((2, rows, 128, width), F32),
            pltpu.VMEM((128, 128), F32),
            pltpu.SMEM((8, 128), jnp.int32),
            pltpu.VMEM((width // 128, levels * rows, 128), F32),
            pltpu.VMEM((width // 128, levels * rows, 128), F32),
            dma,
            dma((2, width // 128)),
        ],
        compiler_params=pltpu.CompilerParams(vmem_limit_bytes=VMEM_LIMIT),
        cost_estimate=pl.CostEstimate(flops=10**10, bytes_accessed=10**7, transcendentals=0),
        name="inner",
    )(beta_prev, low, high, order, bound, part, vert_root, spread, lan, prev)
    vector, coefficients = pl.pallas_call(
        functools.partial(filter_kernel, tiles),
        out_shape=(jax.ShapeDtypeStruct(flat, F32), jax.ShapeDtypeStruct((2,), F32)),
        in_specs=[smem] + [vmem] * 9 + [hbm] * 2,
        out_specs=(hbm, smem),
        scratch_shapes=[
            pltpu.VMEM((width // 128, levels * rows, 128), F32),
            pltpu.VMEM((width // 128, levels * rows, 128), F32),
            pltpu.VMEM((2 * SWEEPS, 128, width), F32),
            pltpu.VMEM((8, 128), F32),
            pltpu.VMEM((tiles, 8, 128), F32),
            dma((2, width // 128)),
            dma((tiles,)), dma((tiles,)),
        ],
        compiler_params=pltpu.CompilerParams(
            collective_id=1, has_side_effects=True, vmem_limit_bytes=VMEM_LIMIT
        ),
        name="filter",
    )(beta_prev, low, mid, high, below, above, inner, sums, spread, spread_halo, lan, prev)
    return vector.reshape(lanczos.shape), coefficients


def solution(mesh):
    placed = (
        P(("ens", "tile")),
        P(("ens", "tile")),
        P(("ens", "tile"), None),
        P(("ens", "tile")),
        P(None, ("ens", "tile")),
        P(None, ("ens", "tile")),
        P(),
        P("tile", None),
        P(None, ("ens", "tile"), None),
        P(None, ("ens", "tile"), None),
        P("ens"),
    )
    return jax.shard_map(
        per_device,
        mesh=mesh,
        in_specs=placed,
        out_specs=(P(None, ("ens", "tile"), None), P("ens")),
        check_vma=False,
    )
```

```python
import functools

import jax
import jax.numpy as jnp
from jax import lax
from jax.experimental import pallas as pl
from jax.experimental.pallas import tpu as pltpu
from jax.sharding import PartitionSpec as P

SWEEPS = 4
GROUP = 256
WINDOW = 3
F32 = jnp.float32
BF16 = jnp.bfloat16
HIGH = lax.Precision.HIGHEST
MESH = pl.DeviceIdType.MESH
VMEM_LIMIT = 56 * 1024 * 1024
ROUTE_LIMIT = 60 * 1024 * 1024
INNER_LIMIT = 56 * 1024 * 1024
FILTER_LIMIT = 32 * 1024 * 1024


def iota(shape, axis):
    return lax.broadcasted_iota(jnp.int32, shape, axis)


def dot_nt(a, b):
    return lax.dot_general(a, b, (((1,), (1,)), ((), ())), preferred_element_type=F32)


def split(x):
    hi = x.astype(BF16).astype(F32)
    return hi, x - hi


def earlier(size):
    return (iota((size, size), 0) < iota((size, size), 1)).astype(BF16)


def greet(tiles, me, ens):
    barrier = pltpu.get_barrier_semaphore()

    def signal(k, carry):
        peer = lax.rem(me + k, tiles)
        pl.semaphore_signal(barrier, inc=1, device_id=(ens, peer), device_id_type=MESH)
        return carry

    lax.fori_loop(1, tiles, signal, 0)
    return barrier


def lifted(row, width):
    return jnp.broadcast_to(row, (16, width)).astype(BF16)


def offsets(row, width):
    return (jnp.broadcast_to(row, (16, width)) - iota((16, width), 0).astype(F32)).astype(BF16)


def one_hot(diff, count, value):
    zero = jnp.zeros_like(value)
    return jnp.concatenate(
        [jnp.where(diff == BF16(16 * a), value, zero) for a in range(count // 16)], axis=0
    )


def spread_out(key, pay, count):
    zero = jnp.zeros_like(pay)
    return jnp.concatenate([jnp.where(key == BF16(g), pay, zero) for g in range(count)], axis=0)


def route_kernel(
    tiles, cap, dep_hbm, wgt_hbm, own_hbm, lev_hbm, col_hbm, itp_hbm, spread_hbm, out_ref, spr_ref,
    dep_ref, wgt_ref, own_ref, lev_ref, col_ref, itp_ref, spread_ref, load_sem, left_ref, right_ref, send_ref, send_sem, recv_sem, spr_send, spr_recv,
):
    me, ens = lax.axis_index("tile"), lax.axis_index("ens")
    for side, edge in enumerate((0, tiles - 1)):

        @pl.when(me == edge)
        def _():
            spr_ref[side] = jnp.zeros(spr_ref.shape[1:], F32)

    loads = [
        pltpu.make_async_copy(src, dst, load_sem.at[i])
        for i, (src, dst) in enumerate((
            (own_hbm, own_ref), (dep_hbm, dep_ref), (wgt_hbm, wgt_ref), (lev_hbm, lev_ref),
            (col_hbm, col_ref), (itp_hbm, itp_ref), (spread_hbm, spread_ref),
        ))
    ]
    for load in loads:
        load.start()
    barrier = greet(tiles, me, ens)
    obs = dep_ref.shape[1]
    size = min(256, cap)
    per = cap // size
    upper = earlier(size)
    base = jnp.zeros((tiles, 1), F32)
    ones = jnp.ones((16, size), BF16)
    for load in loads:
        load.wait()
    for c in range(obs // size):
        at = pl.ds(c * size, size)
        own = own_ref[:, at]
        hot = own == iota((tiles, size), 0)
        one = hot.astype(F32)
        before = jnp.dot(one.astype(BF16), upper, preferred_element_type=F32)
        rank = jnp.sum(one * (before + base), axis=0, keepdims=True).astype(jnp.int32)
        base = base + jnp.sum(one, axis=1, keepdims=True)
        value = itp_ref[:, at] * (wgt_ref[:, at] * dep_ref[:, at])
        hi, lo = split(value)
        cell = col_ref[0:1, at]
        pay = jnp.concatenate(
            [
                hi, lev_ref[:, at].astype(F32), (cell // 256).astype(F32),
                lax.rem(cell, 256).astype(F32), jnp.ones((1, size), F32),
                lo, jnp.zeros((4, size), F32),
            ],
            axis=0,
        ).astype(BF16)
        key = lifted((own * per + rank // size).astype(F32), size)
        left_ref[:, at] = spread_out(key, pay, tiles * per)
        right_ref[:, at] = one_hot(offsets(lax.rem(rank, size).astype(F32), size), size, ones)
    total = dot_nt(left_ref[...], right_ref[...])
    for t in range(tiles):
        for h in range(per):
            k = (t * per + h) * 16
            send_ref[t, :, h * size : (h + 1) * size] = total[k : k + 8] + total[k + 8 : k + 16]
    pl.semaphore_wait(barrier, tiles - 1)

    def spr_copy(side):
        peer = jnp.clip(me + 1 if side == 0 else me - 1, 0, tiles - 1)
        return pltpu.make_async_remote_copy(
            src_ref=spread_ref,
            dst_ref=spr_ref.at[side],
            send_sem=spr_send.at[side],
            recv_sem=spr_recv.at[side],
            device_id=(ens, peer),
            device_id_type=MESH,
        )

    def copy_to(k):
        peer = lax.rem(me + k, tiles)
        return pltpu.make_async_remote_copy(
            src_ref=send_ref.at[peer],
            dst_ref=out_ref.at[me],
            send_sem=send_sem.at[k],
            recv_sem=recv_sem.at[k],
            device_id=(ens, peer),
            device_id_type=MESH,
        )

    def start(k, carry):
        copy_to(k).start()
        return carry

    def wait(k, carry):
        copy_to(k).wait()
        return carry

    lax.fori_loop(1, tiles, start, 0)
    sends = (me < tiles - 1, me > 0)
    for side in range(2):
        pl.when(sends[side])(spr_copy(side).start)
    out_ref[me] = send_ref[me]
    lax.fori_loop(1, tiles, wait, 0)
    for side in range(2):
        pl.when(sends[1 - side])(spr_copy(side).wait_recv)
        pl.when(sends[side])(spr_copy(side).wait_send)


def load_root(root_ref, vert_ref):
    levels = root_ref.shape[0]
    vert_ref[...] = jnp.zeros_like(vert_ref)
    vert_ref[:levels, :levels] = root_ref[...]
    return vert_ref[...].T


def add_rows(low, high, edge_ref, sort_ref, grad_ref):
    ones = jnp.ones((16, GROUP), BF16)

    def one_row(r, carry):
        first, last = edge_ref[0, r], edge_ref[1, r]
        begin = first // GROUP
        end = jnp.where(last > first, (last + GROUP - 1) // GROUP, begin)

        def window(i, inner):
            hots, lefts = [], []
            for w in range(WINDOW):
                block = sort_ref[begin + i * WINDOW + w]
                value = jnp.where(block[5:6] == r.astype(F32), block, 0.0)
                hots.append(one_hot(offsets(block[6:7], GROUP), 256, ones))
                diff = offsets(block[4:5], GROUP)
                for low in (0, 8):
                    lefts.append(jnp.concatenate(
                        [one_hot(diff, 128, lifted(value[low + k : low + k + 1], GROUP)) for k in range(4)],
                        axis=0,
                    ))
            right = jnp.concatenate([h for h in hots for low in range(2)], axis=1)
            part = dot_nt(jnp.concatenate(lefts, axis=1), right)
            for k in range(4):
                grad_ref[k % 2, r + k // 2] += part[k * 128 : (k + 1) * 128]
            return inner

        lax.fori_loop(0, (end - begin + WINDOW - 1) // WINDOW, window, 0)
        return carry

    lax.fori_loop(low, high, one_row, 0)


def levels_of(root, grad_ref, x):
    grad = grad_ref[0, x] + pltpu.roll(grad_ref[1, x], 1, 1)
    return jnp.dot(root, grad, precision=HIGH, preferred_element_type=F32)


def scatter_kernel(
    recv_ref, root_hbm, low_ref, high_ref, sort_ref, bound_ref, part_ref,
    root_ref, root_sem, left_ref, right_ref, grad_ref, vert_ref, edge_ref, sem,
):
    load = pltpu.make_async_copy(root_hbm, root_ref, root_sem)
    load.start()
    tiles, _, cap = recv_ref.shape
    rows = grad_ref.shape[1]
    wide = SWEEPS
    slots = tiles * cap
    groups = slots // GROUP
    size = min(256, cap)
    per = cap // size
    upper = earlier(size)
    grad_ref[...] = jnp.zeros_like(grad_ref)
    ones = jnp.ones((16, GROUP), BF16)

    def hot_of(s, c):
        at = pl.ds(c * size, size)
        row, valid = recv_ref[s, 5:6, at], recv_ref[s, 7:8, at]
        key = jnp.where(valid > 0.5, row, -1.0).astype(jnp.int32)
        return (key == iota((rows, size), 0)).astype(F32)

    counts = jnp.zeros((rows, 1), F32)
    for s in range(tiles):
        for c in range(per):
            counts = counts + jnp.sum(hot_of(s, c), axis=1, keepdims=True)
    sub, lane = iota((rows, 128), 0), iota((rows, 128), 1)
    as_row = jnp.sum(jnp.where(sub == lane, counts, 0.0), axis=0, keepdims=True)
    base = jnp.sum(jnp.where(lane < sub, as_row, 0.0), axis=1, keepdims=True)
    start_row = jnp.sum(jnp.where(sub == lane, base, 0.0), axis=0, keepdims=True)
    bound_ref[...] = jnp.concatenate(
        [start_row, start_row + as_row, jnp.zeros((6, 128), F32)], axis=0
    ).astype(jnp.int32)
    bounds = pltpu.make_async_copy(bound_ref, edge_ref, sem)
    bounds.start()
    for s in range(tiles):
        for c in range(per):
            at = pl.ds(c * size, size)
            to = pl.ds((s * per + c) * size, size)
            one = hot_of(s, c)
            before = jnp.dot(one.astype(BF16), upper, preferred_element_type=F32)
            pos = jnp.sum(one * (before + base), axis=0, keepdims=True).astype(jnp.int32)
            base = base + jnp.sum(one, axis=1, keepdims=True)
            hi, lo = split(recv_ref[s, :, at])
            pay = jnp.concatenate([hi, lo], axis=0).astype(BF16)
            left_ref[:, to] = spread_out(lifted((pos // GROUP).astype(F32), size), pay, groups)
            right_ref[:, to] = one_hot(
                offsets(lax.rem(pos, GROUP).astype(F32), size), GROUP, ones[:, :size]
            )
    total = dot_nt(left_ref[...], right_ref[...])
    sort_ref[:groups] = total.reshape(groups, 16, GROUP)
    for w in range(groups, sort_ref.shape[0]):
        sort_ref[w] = jnp.zeros((16, GROUP), F32)
    bounds.wait()

    add_rows(0, wide, edge_ref, sort_ref, grad_ref)
    add_rows(rows - wide - 1, rows - 1, edge_ref, sort_ref, grad_ref)
    load.wait()
    root = load_root(root_ref, vert_ref)
    for x in range(wide):
        low_ref[x] = levels_of(root, grad_ref, x)
        high_ref[x] = levels_of(root, grad_ref, rows - wide + x)
    for dj in range(2):
        part_ref[0, dj] = grad_ref[dj, wide]
        part_ref[1, dj] = grad_ref[dj, rows - wide - 1]


def sweep_rows(field, spread_of, low, high):
    width = field[low].shape[1]
    for sweep in range(SWEEPS):
        pushed = {x: spread_of(x) * field[x] for x in range(low, high)}
        low, high = low + 1, high - 1
        for x in range(low, high):
            p = pushed[x]
            field[x] = field[x] + (
                pushed[x + 1] + pushed[x - 1]
                + pltpu.roll(p, 1, 1) + pltpu.roll(p, width - 1, 1) - 4.0 * p
            )
    return field


def strided(ref, begin, count, x, rows):
    where = pl.ds(begin * rows + x, count, stride=rows)
    return jnp.concatenate([ref[h, where, :] for h in range(ref.shape[0])], axis=1)


def add_sums(sum_ref, pairs):
    dl, ll, dd = (sum(v) for v in zip(*[(d * l, l * l, d * d) for d, l in pairs]))
    for i, value in enumerate((dl, ll, dd)):
        row = jnp.sum(value, axis=0, keepdims=True)
        sum_ref[i : i + 1, :] += row[:, :128] + row[:, 128:]


def for_levels(levels, chunk):
    full = levels // 8
    pl.loop(0, full)(lambda c: chunk(pl.multiple_of(c * 8, 8), 8))
    if levels % 8:
        chunk(full * 8, levels % 8)


def loads_of(pairs, sem):
    return [
        pltpu.make_async_copy(src.at[:, pl.ds(h * 128, 128)], dst.at[h], sem.at[i, h])
        for i, (src, dst) in enumerate(pairs)
        for h in range(dst.shape[0])
    ]


def inner_kernel(
    beta_ref, low_ref, high_ref, sort_ref, bound_ref, part_ref, root_hbm, spread_hbm, lan_hbm, prev_hbm,
    mid_ref, diff_ref, sum_ref, root_ref, spread_ref, small_sem, grad_ref, vert_ref, edge_ref, lan_ref, prev_ref, sem, local_sem,
):
    rows = spread_ref.shape[0]
    levels = root_ref.shape[0]
    wide = SWEEPS
    bounds = pltpu.make_async_copy(bound_ref, edge_ref, sem)
    bounds.start()
    small = [
        pltpu.make_async_copy(root_hbm, root_ref, small_sem.at[0]),
        pltpu.make_async_copy(spread_hbm, spread_ref, small_sem.at[1]),
    ]
    for load in small:
        load.start()
    loads = loads_of(((lan_hbm, lan_ref), (prev_hbm, prev_ref)), local_sem)
    for load in loads:
        load.start()
    for dj in range(2):
        grad_ref[dj, wide] = part_ref[0, dj]
        grad_ref[dj, rows - wide - 1] = part_ref[1, dj]
        for x in range(wide + 1, rows - wide - 1):
            grad_ref[dj, x] = jnp.zeros(grad_ref.shape[2:], F32)
    bounds.wait()
    add_rows(wide, rows - wide - 1, edge_ref, sort_ref, grad_ref)
    for load in small:
        load.wait()
    root = load_root(root_ref, vert_ref)
    for x in range(wide, rows - wide):
        mid_ref[x - wide] = levels_of(root, grad_ref, x)
    for load in loads:
        load.wait()
    beta_prev = beta_ref[0]
    sum_ref[...] = jnp.zeros_like(sum_ref)

    def chunk(begin, count):
        at = pl.ds(begin, count)
        field = {x: low_ref[x, at, :] for x in range(wide)}
        field.update({x: mid_ref[x - wide, at, :] for x in range(wide, rows - wide)})
        field.update({x: high_ref[x - rows + wide, at, :] for x in range(rows - wide, rows)})
        field = sweep_rows(field, lambda x: spread_ref[x : x + 1, :], 0, rows)
        pairs = []
        for x in range(wide, rows - wide):
            diff = field[x] - beta_prev * strided(prev_ref, begin, count, x, rows)
            diff_ref[x - wide, at, :] = diff
            pairs.append((diff, strided(lan_ref, begin, count, x, rows)))
        add_sums(sum_ref, pairs)

    for_levels(levels, chunk)


def filter_kernel(
    tiles, beta_ref, low_ref, mid_ref, high_ref, below_ref, above_ref, inner_ref, part_ref, spread_hbm, spr_ref,
    lan_hbm, prev_hbm, out_hbm, coef_ref, spread_ref, spread_sem,
    lan_ref, prev_ref, diff_ref, sum_ref, all_ref, local_sem, sum_send, sum_recv,
):
    me, ens = lax.axis_index("tile"), lax.axis_index("ens")
    rows, width = spread_ref.shape
    levels = lan_hbm.shape[0] // rows
    wide = SWEEPS
    loads = [pltpu.make_async_copy(spread_hbm, spread_ref, spread_sem)]
    loads += loads_of(((lan_hbm, lan_ref), (prev_hbm, prev_ref)), local_sem)
    for load in loads:
        load.start()
    barrier = greet(tiles, me, ens)
    for load in loads:
        load.wait()
    beta_prev = beta_ref[0]
    sum_ref[...] = part_ref[...]

    def spread_row(x):
        if x < 0:
            return spr_ref[0, rows + x : rows + x + 1, :]
        if x >= rows:
            return spr_ref[1, x - rows : x - rows + 1, :]
        return spread_ref[x : x + 1, :]

    def field_row(x, at):
        for ref, begin in ((below_ref, -wide), (low_ref, 0), (mid_ref, wide), (high_ref, rows - wide), (above_ref, rows)):
            if begin <= x < begin + ref.shape[0]:
                return ref[x - begin, at, :]

    def chunk(begin, count):
        at = pl.ds(begin, count)
        pairs = []
        for first in (0, rows - wide):
            span = (first - wide, first + 2 * wide)
            field = sweep_rows({x: field_row(x, at) for x in range(*span)}, spread_row, *span)
            for x in range(first, first + wide):
                diff = field[x] - beta_prev * strided(prev_ref, begin, count, x, rows)
                diff_ref[x % (2 * wide), at, :] = diff
                pairs.append((diff, strided(lan_ref, begin, count, x, rows)))
        add_sums(sum_ref, pairs)

    for_levels(levels, chunk)
    pl.semaphore_wait(barrier, tiles - 1)

    def share(k):
        peer = lax.rem(me + k, tiles)
        return pltpu.make_async_remote_copy(
            src_ref=sum_ref,
            dst_ref=all_ref.at[me],
            send_sem=sum_send.at[k],
            recv_sem=sum_recv.at[k],
            device_id=(ens, peer),
            device_id_type=MESH,
        )

    def start(k, carry):
        share(k).start()
        return carry

    def wait(k, carry):
        share(k).wait()
        return carry

    lax.fori_loop(1, tiles, start, 0)
    all_ref[me] = sum_ref[...]
    lax.fori_loop(1, tiles, wait, 0)
    sums = jnp.sum(jnp.sum(all_ref[...], axis=0), axis=1, keepdims=True)
    dl, ll, dd = sums[0:1], sums[1:2], sums[2:3]
    extra = dl / ll
    beta = jnp.sqrt(jnp.maximum(dd - extra * dl, 0.0) / ll + 1e-06)
    coef_ref[0] = (1.0 + extra)[0, 0]
    coef_ref[1] = beta[0, 0]
    scale = 1.0 / beta

    def finish(begin, count):
        for x in range(rows):
            where = pl.ds(begin * rows + x, count, stride=rows)
            for h in range(width // 128):
                at = (pl.ds(begin, count), pl.ds(h * 128, 128))
                if wide <= x < rows - wide:
                    diff = inner_ref[x - wide, *at]
                else:
                    diff = diff_ref[x % (2 * wide), *at]
                prev_ref[h, where, :] = (diff - extra * lan_ref[h, where, :]) * scale

    for_levels(levels, finish)
    stores = [
        pltpu.make_async_copy(prev_ref.at[h], out_hbm.at[:, pl.ds(h * 128, 128)], local_sem.at[0, h])
        for h in range(width // 128)
    ]
    for store in stores:
        store.start()
    for store in stores:
        store.wait()


def per_device(
    departure, obs_weight, owner_id, obs_level, columns, interp_weight, vert_root,
    spread, lanczos, previous, beta_prev,
):
    tiles = lax.axis_size("tile")
    obs = departure.shape[0]
    cap = 2 * obs // tiles
    rows, width = spread.shape
    levels = lanczos.shape[0]
    size = min(256, cap)
    slots = tiles * cap
    vmem = pl.BlockSpec(memory_space=pltpu.VMEM)
    smem = pl.BlockSpec(memory_space=pltpu.SMEM)
    hbm = pl.BlockSpec(memory_space=pl.ANY)
    far = pl.BlockSpec(memory_space=pltpu.HBM)
    dma = pltpu.SemaphoreType.DMA
    received, spread_halo = pl.pallas_call(
        functools.partial(route_kernel, tiles, cap),
        out_shape=(
            jax.ShapeDtypeStruct((tiles, 8, cap), F32),
            jax.ShapeDtypeStruct((2, rows, width), F32),
        ),
        in_specs=[far] * 7,
        out_specs=(vmem, vmem),
        scratch_shapes=[
            pltpu.VMEM((1, obs), F32),
            pltpu.VMEM((1, obs), F32),
            pltpu.VMEM((1, obs), jnp.int32),
            pltpu.VMEM((1, obs), jnp.int32),
            pltpu.VMEM(columns.shape, jnp.int32),
            pltpu.VMEM(interp_weight.shape, F32),
            pltpu.VMEM(spread.shape, F32),
            dma((7,)),
            pltpu.VMEM((tiles * cap // size * 16, obs), BF16),
            pltpu.VMEM((size, obs), BF16),
            pltpu.VMEM((tiles, 8, cap), F32),
            dma((tiles,)), dma((tiles,)), dma((2,)), dma((2,)),
        ],
        compiler_params=pltpu.CompilerParams(
            collective_id=0, has_side_effects=True, vmem_limit_bytes=ROUTE_LIMIT
        ),
        name="route",
    )(
        departure.reshape(1, obs), obs_weight.reshape(1, obs), owner_id.reshape(1, obs),
        obs_level.reshape(1, obs), columns, interp_weight, spread,
    )
    flat = (levels * rows, width)
    lan, prev = lanczos.reshape(flat), previous.reshape(flat)
    edge = jax.ShapeDtypeStruct((SWEEPS, 128, width), F32)
    middle = jax.ShapeDtypeStruct((rows - 2 * SWEEPS, 128, width), F32)
    low, high, order, bound, part = pl.pallas_call(
        scatter_kernel,
        out_shape=(
            edge,
            edge,
            jax.ShapeDtypeStruct((slots // GROUP + WINDOW - 1, 16, GROUP), F32),
            jax.ShapeDtypeStruct((8, 128), jnp.int32),
            jax.ShapeDtypeStruct((2, 2, 128, width), F32),
        ),
        in_specs=[vmem, far],
        out_specs=[vmem] * 5,
        scratch_shapes=[
            pltpu.VMEM(vert_root.shape, F32),
            dma,
            pltpu.VMEM((slots // GROUP * 16, slots), BF16),
            pltpu.VMEM((GROUP, slots), BF16),
            pltpu.VMEM((2, rows, 128, width), F32),
            pltpu.VMEM((128, 128), F32),
            pltpu.SMEM((8, 128), jnp.int32),
            dma,
        ],
        compiler_params=pltpu.CompilerParams(vmem_limit_bytes=VMEM_LIMIT),
        name="scatter",
    )(received, vert_root)
    up = [(i, i + 1) for i in range(tiles - 1)]
    below = lax.ppermute(high, "tile", up)
    above = lax.ppermute(low, "tile", [(j, i) for i, j in up])
    mid, inner, sums = pl.pallas_call(
        inner_kernel,
        out_shape=(middle, middle, jax.ShapeDtypeStruct((8, 128), F32)),
        in_specs=[smem] + [vmem] * 5 + [far] * 4,
        out_specs=[vmem] * 3,
        scratch_shapes=[
            pltpu.VMEM(vert_root.shape, F32),
            pltpu.VMEM(spread.shape, F32),
            dma((2,)),
            pltpu.VMEM((2, rows, 128, width), F32),
            pltpu.VMEM((128, 128), F32),
            pltpu.SMEM((8, 128), jnp.int32),
            pltpu.VMEM((width // 128, levels * rows, 128), F32),
            pltpu.VMEM((width // 128, levels * rows, 128), F32),
            dma,
            dma((2, width // 128)),
        ],
        compiler_params=pltpu.CompilerParams(vmem_limit_bytes=INNER_LIMIT),
        cost_estimate=pl.CostEstimate(flops=10**10, bytes_accessed=10**7, transcendentals=0),
        name="inner",
    )(beta_prev, low, high, order, bound, part, vert_root, spread, lan, prev)
    vector, coefficients = pl.pallas_call(
        functools.partial(filter_kernel, tiles),
        out_shape=(jax.ShapeDtypeStruct(flat, F32), jax.ShapeDtypeStruct((2,), F32)),
        in_specs=[smem] + [vmem] * 7 + [far] + [vmem] + [far] * 2,
        out_specs=(hbm, smem),
        scratch_shapes=[
            pltpu.VMEM(spread.shape, F32),
            dma,
            pltpu.VMEM((width // 128, levels * rows, 128), F32),
            pltpu.VMEM((width // 128, levels * rows, 128), F32),
            pltpu.VMEM((2 * SWEEPS, 128, width), F32),
            pltpu.VMEM((8, 128), F32),
            pltpu.VMEM((tiles, 8, 128), F32),
            dma((2, width // 128)),
            dma((tiles,)), dma((tiles,)),
        ],
        compiler_params=pltpu.CompilerParams(
            collective_id=1, has_side_effects=True, vmem_limit_bytes=FILTER_LIMIT
        ),
        name="filter",
    )(beta_prev, low, mid, high, below, above, inner, sums, spread, spread_halo, lan, prev)
    return vector.reshape(lanczos.shape), coefficients


def solution(mesh):
    placed = (
        P(("ens", "tile")),
        P(("ens", "tile")),
        P(("ens", "tile"), None),
        P(("ens", "tile")),
        P(None, ("ens", "tile")),
        P(None, ("ens", "tile")),
        P(),
        P("tile", None),
        P(None, ("ens", "tile"), None),
        P(None, ("ens", "tile"), None),
        P("ens"),
    )
    return jax.shard_map(
        per_device,
        mesh=mesh,
        in_specs=placed,
        out_specs=(P(None, ("ens", "tile"), None), P("ens")),
        check_vma=False,
    )
```
